256 devices in a mesh: opt: 2 (over z_hi), dp: 8 (over x, core), tensor: 16 (over z_lo, y).
Axes of the slice: x: 4, y: 4, z: 8 (z_hi: 2, z_lo: 4; z = z_hi * 4 + z_lo), core: 2. Of those that a mesh axis runs over, the one named last changes fastest.
Arguments:
- tokens: bfloat16 [4096, 4096], P(('opt', 'dp')), may hold values from -6 to 6
- grad_hidden: bfloat16 [4096, 14336], P(('opt', 'dp'), 'tensor'), may hold values from -6 to 6
- weight_codes: bfloat16 [32, 128, 28672], P(('opt', 'dp'), None, 'tensor'), may hold values from -96 to 96
- scales: float32 [32, 224], P(('opt', 'dp'), 'tensor'), may hold values from 0.00048828125 to 0.001953125
- master: float32 [4096, 28672], P(('opt', 'dp'), 'tensor'), may hold values from -0.09375 to 0.09375
- first_moment: bfloat16 [4096, 28672], P(('opt', 'dp'), 'tensor'), may hold values from -6 to 6
- second_moment: bfloat16 [4096, 28672], P(('opt', 'dp'), 'tensor'), may hold values from 0.049804688 to 2
Outputs:
- hidden: bfloat16 [4096, 14336], P(('opt', 'dp'), 'tensor')
- grad_tokens: bfloat16 [4096, 4096], P(('opt', 'dp'), 'tensor')
- new_master: float32 [4096, 28672], P(('opt', 'dp'), 'tensor')
- new_first: bfloat16 [4096, 28672], P(('opt', 'dp'), 'tensor')
- new_second: bfloat16 [4096, 28672], P(('opt', 'dp'), 'tensor')
The draws below stay inside these ranges and needn't reach their ends.
All inputs are finite; a program needn't handle non-finite values.
Results may differ from the reference program's by a relative error of at most 0.04.
Values may be sent and summed in bfloat16 or wider, within the bound.
No kernel may reach another device: no remote copies, remote signals or barrier semaphores. Data moves between devices by JAX's collectives and lax.ppermute only.
A program may use at most 192 MiB of HBM per device.

```python
import math
import jax
import jax.numpy as jnp
from jax import lax

D = 4096
FF = 14336
BLOCK = 128
TOKENS = 4096
N_OPT = 2
N_DP = 8
N_TENSOR = 16


def spiked(values, stream_key, source, target, parts, factor):
    owner, partner = [(jnp.arange(values.shape[position]) // (values.shape[position] // parts)).reshape([-1 if axis == position else 1 for axis in range(values.ndim)]) for position in (source, target)]
    chosen = jax.random.permutation(stream_key, parts)[partner]
    strong = (owner == chosen) | (owner == (partner + parts // 2) % parts)
    return jnp.where(strong, factor * values, values)


def level_of(stream_key, dims, shards, smallest, largest):
    def one(axis_at, blocks):
        heights = jax.random.uniform(jax.random.fold_in(jax.random.fold_in(stream_key, 6), axis_at), (blocks,), jnp.float32, smallest / len(shards), largest / len(shards))
        return jnp.repeat(jnp.exp(heights), dims[axis_at] // blocks).reshape((-1,) + (1,) * (len(dims) - axis_at - 1))

    factor_of = one(*shards[0])
    for cut in shards[1:]:
        factor_of = factor_of * one(*cut)
    return factor_of


def normal_values(own_key, dims, scale, reach, pieces=(), held_as=jnp.bfloat16):
    entries = jax.random.normal(own_key, dims, jnp.float32) * scale
    if len(pieces) > 0:
        entries = level_of(own_key, dims, pieces, -0.22, 0.18) * entries
    return jnp.clip(entries, min=-reach, max=reach).astype(held_as)


def gaussian_with(rng, dims, spread, reach, cuts, heavy, kind=jnp.bfloat16):
    drawn = spread * jax.random.normal(rng, dims, jnp.float32)
    if cuts:
        drawn = drawn * level_of(rng, dims, cuts, -0.22, 0.18)
    return jnp.clip(spiked(drawn, jax.random.fold_in(rng, 3), *heavy), -reach, reach).astype(kind)


def setup_inputs(seed: int = 0) -> dict:
    key_list = jax.random.split(jax.random.key(seed), 8)
    tokens = gaussian_with(key_list[0], (TOKENS, D), 1.0, 6.0, ((0, 16),), (0, 1, 16, 2.0))
    grad_hidden = normal_values(key_list[1], (TOKENS, FF), 1.0, 6.0, ((0, 16), (1, 16)))
    weight_codes = normal_values(key_list[2], (D // BLOCK, BLOCK, 2 * FF), 16.0, 96.0, ((0, 16), (2, 16)))
    scales = jnp.clip(jnp.exp(math.log(0.001953125) - 1.3862944 * jax.random.uniform(key_list[3], (D // BLOCK, 2 * FF // BLOCK), jnp.float32) ** level_of(key_list[3], (D // BLOCK, 2 * FF // BLOCK), ((0, 16), (1, 16)), -0.2, 0.2)), 0.00048828125, 0.001953125)
    master = normal_values(key_list[4], (D, 2 * FF), D ** -0.5, 0.09375, ((0, 16), (1, 16)), jnp.float32)
    first_moment = normal_values(key_list[5], (D, 2 * FF), 0.5, 6.0, ((0, 16), (1, 16)))
    second_moment = jnp.clip(jnp.exp(math.log(2.0) - 3.6927934 * jax.random.uniform(key_list[6], (D, 2 * FF), jnp.float32) ** level_of(key_list[6], (D, 2 * FF), ((0, 16), (1, 16)), -0.2, 0.2)), 0.049804688, 2.0).astype(jnp.bfloat16)
    return {"tokens": tokens, "grad_hidden": grad_hidden, "weight_codes": weight_codes, "scales": scales, "master": master, "first_moment": first_moment, "second_moment": second_moment}


def dequantize(weight_codes, scales):
    blocks, inner_rows, columns = weight_codes.shape
    scaled = weight_codes.astype(jnp.float32).reshape(blocks, inner_rows, columns // inner_rows, inner_rows) * scales[:, None, :, None]
    return scaled.reshape(blocks * inner_rows, columns).astype(jnp.bfloat16)

def adam_update(grads, master, first_moment, second_moment):
    adam_count = 20.0
    moment_one = 0.9 * first_moment.astype(jnp.float32) + 0.1 * grads
    moment_two = 0.95 * second_moment.astype(jnp.float32) + 0.05 * grads * grads
    fix_one = 1.0 - 0.9 ** adam_count
    fix_two = 1.0 - 0.95 ** adam_count
    direction = moment_one / fix_one / (jnp.sqrt(moment_two / fix_two) + 1e-08)
    new_master = master - 0.001 * (direction + 0.1 * master)
    return (new_master, moment_one.astype(jnp.bfloat16), moment_two.astype(jnp.bfloat16))

def rounded(values):
    narrow = lax.optimization_barrier(values.astype(jnp.bfloat16))
    return narrow.astype(jnp.float32)

def reference(tokens, grad_hidden, weight_codes, scales, master, first_moment, second_moment):
    weights = dequantize(weight_codes, scales)
    group_width = FF // N_TENSOR
    projected = jnp.dot(tokens, weights, preferred_element_type=jnp.float32)
    grouped = projected.reshape(TOKENS, N_TENSOR, 2, group_width)
    gate_part = grouped[:, :, 0, :].reshape(TOKENS, FF)
    up_part = grouped[:, :, 1, :].reshape(TOKENS, FF)
    sigmoid_gate = jax.nn.sigmoid(gate_part)
    activated = gate_part * sigmoid_gate
    hidden = (activated * up_part).astype(jnp.bfloat16)
    upstream = grad_hidden.astype(jnp.float32)
    grad_gate = upstream * up_part * sigmoid_gate * (1.0 + gate_part * (1.0 - sigmoid_gate))
    grad_up = upstream * activated
    grad_proj = jnp.stack([grad_gate.reshape(TOKENS, N_TENSOR, group_width), grad_up.reshape(TOKENS, N_TENSOR, group_width)], axis=2)
    grad_proj = grad_proj.reshape(TOKENS, 2 * FF).astype(jnp.bfloat16)
    proj_groups = grad_proj.reshape(TOKENS, N_TENSOR, 2 * group_width).transpose(1, 0, 2)
    weight_groups = weights.reshape(D, N_TENSOR, 2 * group_width).transpose(1, 0, 2)

    def token_term(running, operands):
        partial_value = lax.dot_general(operands[0], operands[1], (((1,), (1,)), ((), ())), preferred_element_type=jnp.float32)
        return (running + rounded(partial_value), None)
    summed, _ = lax.scan(token_term, jnp.zeros((TOKENS, D), jnp.float32), (proj_groups, weight_groups))
    grad_tokens = summed.astype(jnp.bfloat16)
    owner_groups = N_OPT * N_DP
    tok_dev = TOKENS // owner_groups
    grad_scale = 1.0 / math.sqrt(TOKENS)

    def weight_term(running, operands):
        partial_value = lax.dot_general(operands[0], operands[1], (((0,), (0,)), ((), ())), preferred_element_type=jnp.float32) * grad_scale
        return (running + rounded(partial_value), None)
    grads, _ = lax.scan(weight_term, jnp.zeros((D, 2 * FF), jnp.float32), (tokens.reshape(owner_groups, tok_dev, D), grad_proj.reshape(owner_groups, tok_dev, 2 * FF)))
    new_master, new_first, new_second = adam_update(grads, master, first_moment, second_moment)
    return (hidden, grad_tokens, new_master, new_first, new_second)
```

```python
import jax
import jax.numpy as jnp
from jax import lax
from jax.experimental import pallas as pl
from jax.experimental.pallas import tpu as pltpu
from jax.sharding import PartitionSpec as P

F32 = jnp.float32
BF16 = jnp.bfloat16
OT = ("opt", "tensor")
VMEM = pl.BlockSpec(memory_space=pltpu.VMEM)
SMEM = pl.BlockSpec(memory_space=pltpu.SMEM)
LIMIT = 48 * 1024 * 1024

X_GROUPS = [[0, 2, 4, 6], [1, 3, 5, 7]]
EIGHTHS = [list(range(8)), list(range(8, 16))]


def along_x(a, step):
    return lax.ppermute(a, "dp", [(x * 2 + c, (x + step) % 4 * 2 + c) for x in range(4) for c in range(2)])


def other_core(a):
    return lax.ppermute(a, "dp", [(i, i ^ 1) for i in range(8)])


def other_opt(a):
    return lax.ppermute(a, "opt", [(0, 1), (1, 0)])


def along_y(a, step):
    return lax.ppermute(a, "tensor", [(z * 4 + y, z * 4 + (y + step) % 4) for z in range(4) for y in range(4)])


def along_z(a, step):
    return lax.ppermute(a, OT, [(z * 4 + y, (z + step) % 8 * 4 + y) for z in range(8) for y in range(4)])


def params():
    return pltpu.CompilerParams(vmem_limit_bytes=LIMIT)


def low_lanes(shape):
    return lax.broadcasted_iota(jnp.int32, shape, 1) < 64


def prepare_kernel(opt_ref, scale_ref, code_ref, own_ref, send_ref):
    first = opt_ref[0] == 0
    low = low_lanes((128, 128))

    def put(rows, at, half0, half1):
        own_ref[rows, at : at + 128] = jnp.where(first, half0, half1).astype(BF16)
        send_ref[rows, at : at + 128] = jnp.where(first, half1, half0).astype(BF16)

    for b in range(2):
        rows = slice(b * 128, b * 128 + 128)

        def tile(j):
            return code_ref[b, :, j * 128 : j * 128 + 128].astype(F32) * scale_ref[b, j]

        for part in range(2):
            for j in range(3):
                put(rows, part * 384 + j * 128, tile(part * 7 + j), tile(part * 7 + 4 + j))
        gate, up = tile(3), tile(10)
        put(
            rows,
            768,
            jnp.where(low, gate, pltpu.roll(up, 64, 1)),
            jnp.where(low, pltpu.roll(gate, 64, 1), up),
        )


def prepare(opt, scales, codes):
    out = jax.ShapeDtypeStruct((256, 896), BF16)
    return pl.pallas_call(
        prepare_kernel,
        out_shape=(out, out),
        in_specs=[SMEM, SMEM, VMEM],
        out_specs=(VMEM, VMEM),
        compiler_params=params(),
        cost_estimate=pl.CostEstimate(flops=1 << 19, bytes_accessed=1 << 21, transcendentals=0),
    )(opt, scales, codes)


def split_kernel(core_ref, keep_in, send_in, keep_ref, send_ref):
    keep_ref[...] = keep_in[...]
    send_ref[...] = send_in[...]


def split_tokens(core, tokens):
    out = jax.ShapeDtypeStruct((256, 2048), BF16)
    return pl.pallas_call(
        split_kernel,
        out_shape=(out, out),
        grid_spec=pltpu.PrefetchScalarGridSpec(
            num_scalar_prefetch=1,
            grid=(8,),
            in_specs=[
                pl.BlockSpec((256, 256), lambda i, core: (0, 2 * i + core[0])),
                pl.BlockSpec((256, 256), lambda i, core: (0, 2 * i + 1 - core[0])),
            ],
            out_specs=(
                pl.BlockSpec((256, 256), lambda i, core: (0, i)),
                pl.BlockSpec((256, 256), lambda i, core: (0, i)),
            ),
        ),
        compiler_params=params(),
        cost_estimate=pl.CostEstimate(flops=0, bytes_accessed=1 << 22, transcendentals=0),
    )(core, tokens, tokens)


def project_kernel(at_ref, tok_ref, *refs):
    pieces, own_ref, send_ref = refs[:-2], refs[-2], refs[-1]
    for half in range(2):
        rows = slice(half * 256, half * 256 + 256)
        total = None
        for i, piece in enumerate(pieces):
            depth = piece.shape[0]
            columns = pl.ds(pl.multiple_of(at_ref[i] * 128, 128), depth)
            term = jnp.dot(tok_ref[rows, columns], piece[...], preferred_element_type=F32)
            total = term if total is None else total + term
        if half == 0:
            own_ref[...] = total
        else:
            send_ref[...] = total.astype(BF16)


def project(at, tok, pieces):
    return pl.pallas_call(
        project_kernel,
        out_shape=(jax.ShapeDtypeStruct((256, 896), F32), jax.ShapeDtypeStruct((256, 896), BF16)),
        in_specs=[SMEM] + [VMEM] * (1 + len(pieces)),
        out_specs=(VMEM, VMEM),
        compiler_params=params(),
        cost_estimate=pl.CostEstimate(flops=2 * 512 * 2048 * 896, bytes_accessed=7 << 20, transcendentals=0),
    )(at, tok, *pieces)


def swiglu_kernel(own_ref, recv_ref, up_grad_ref, hidden_ref, grad_ref):
    def parts(gate, up, upstream):
        s = 1.0 / (1.0 + jnp.exp(-gate))
        act = gate * s
        return act * up, upstream * up * s * (1.0 + gate * (1.0 - s)), upstream * act

    def projected(at):
        return own_ref[:, at : at + 128] + recv_ref[:, at : at + 128].astype(F32)

    for j in range(3):
        at = j * 128
        hidden, grad_gate, grad_up = parts(
            projected(at), projected(384 + at), up_grad_ref[:, at : at + 128].astype(F32)
        )
        hidden_ref[:, at : at + 128] = hidden.astype(BF16)
        grad_ref[:, at : at + 128] = grad_gate.astype(BF16)
        grad_ref[:, 384 + at : 384 + at + 128] = grad_up.astype(BF16)
    mixed = projected(768)
    hidden, grad_gate, grad_up = parts(mixed, pltpu.roll(mixed, 64, 1), up_grad_ref[:, 384:512].astype(F32))
    hidden_ref[:, 384:512] = hidden.astype(BF16)
    grad_ref[:, 768:896] = jnp.where(low_lanes(mixed.shape), grad_gate, pltpu.roll(grad_up, 64, 1)).astype(BF16)


def swiglu(own, recv, up_grad):
    return pl.pallas_call(
        swiglu_kernel,
        out_shape=(jax.ShapeDtypeStruct((256, 512), BF16), jax.ShapeDtypeStruct((256, 896), BF16)),
        in_specs=[VMEM] * 3,
        out_specs=(VMEM, VMEM),
        compiler_params=params(),
        cost_estimate=pl.CostEstimate(flops=256 * 448 * 16, bytes_accessed=5 << 19, transcendentals=256 * 448),
    )(own, recv, up_grad)


def token_grad_kernel(which_ref, block_ref, g0_ref, g1_ref, *refs):
    weights, extra, out_ref = refs[:4], refs[4:-1], refs[-1]
    i = pl.program_id(0)
    for a in range(4):

        @pl.when(which_ref[i] == a)
        def _():
            for half, g_ref in enumerate((g0_ref, g1_ref)):
                rows = slice(half * 256, half * 256 + 256)
                term = lax.dot_general(
                    g_ref[...], weights[a][0], (((1,), (1,)), ((), ())), preferred_element_type=F32
                )
                if extra:
                    term = term + extra[0][0, rows].astype(F32) * jnp.where(i < 2, 1.0, 0.0)
                out_ref[0, rows] = term.astype(BF16)


def token_grad(which, block, g0, g1, weights, extra=None):
    steps = which.shape[0]

    def of(a):
        return lambda i, which, block: (jnp.where(which[i] == a, block[i], 0), 0, 0)

    in_specs = [pl.BlockSpec((256, 896), lambda i, which, block: (0, 0))] * 2
    in_specs += [pl.BlockSpec((1, 256, 896), of(a)) for a in range(4)]
    args = [g0, g1] + [w.reshape(4, 256, 896) for w in weights]
    if extra is not None:
        in_specs.append(pl.BlockSpec((1, 512, 256), lambda i, which, block: (jnp.minimum(i, 1), 0, 0)))
        args.append(extra)
    return pl.pallas_call(
        token_grad_kernel,
        out_shape=jax.ShapeDtypeStruct((steps, 512, 256), BF16),
        grid_spec=pltpu.PrefetchScalarGridSpec(
            num_scalar_prefetch=2,
            grid=(steps,),
            in_specs=in_specs,
            out_specs=pl.BlockSpec((1, 512, 256), lambda i, which, block: (i, 0, 0)),
        ),
        compiler_params=params(),
        cost_estimate=pl.CostEstimate(
            flops=2 * 512 * 896 * 256 * steps, bytes_accessed=steps * 800000 + 1000000, transcendentals=0
        ),
    )(which, block, *args)


def weight_grad_kernel(half_ref, t0_ref, t1_ref, g0, g1, g2, g3, out_ref):
    total = None
    for rows, t_ref, g in ((0, t0_ref, g0), (256, t0_ref, g1), (0, t1_ref, g2), (256, t1_ref, g3)):
        term = lax.dot_general(
            t_ref[rows : rows + 256, :], g[...], (((0,), (0,)), ((), ())), preferred_element_type=F32
        )
        total = term if total is None else total + term
    out_ref[...] = (total * (1.0 / 64.0)).astype(BF16)


def weight_grad(half, t0, t1, grads):
    tok = pl.BlockSpec((512, 256), lambda i, half: (0, half[0] * 4 + i))
    whole = pl.BlockSpec((256, 896), lambda i, half: (0, 0))
    return pl.pallas_call(
        weight_grad_kernel,
        out_shape=jax.ShapeDtypeStruct((1024, 896), BF16),
        grid_spec=pltpu.PrefetchScalarGridSpec(
            num_scalar_prefetch=1,
            grid=(4,),
            in_specs=[tok, tok] + [whole] * 4,
            out_specs=pl.BlockSpec((256, 896), lambda i, half: (i, 0)),
        ),
        compiler_params=params(),
        cost_estimate=pl.CostEstimate(flops=2 * 1024 * 1024 * 896, bytes_accessed=6 << 20, transcendentals=0),
    )(half, t0, t1, *grads)


def adam_kernel(opt_ref, mine_ref, recv_ref, master_ref, m_ref, v_ref, master_out, m_out, v_out):
    first = opt_ref[0] == 0
    low = low_lanes((mine_ref.shape[0], 128))
    fix_one = 1.0 - 0.9**20.0
    fix_two = 1.0 - 0.95**20.0

    def tile(half, at):
        mine, recv = (r[:, at : at + 128].astype(F32) for r in (mine_ref, recv_ref))
        return jnp.where(first, mine, recv) if half == 0 else jnp.where(first, recv, mine)

    mixed0, mixed1 = tile(0, 768), tile(1, 768)
    for j in range(14):
        part, k = divmod(j, 7)
        if k < 3:
            grads = tile(0, part * 384 + k * 128)
        elif k > 3:
            grads = tile(1, part * 384 + (k - 4) * 128)
        elif part == 0:
            grads = jnp.where(low, mixed0, pltpu.roll(mixed1, 64, 1))
        else:
            grads = jnp.where(low, pltpu.roll(mixed0, 64, 1), mixed1)
        at = slice(j * 128, j * 128 + 128)
        master = master_ref[:, at]
        one = 0.9 * m_ref[:, at].astype(F32) + 0.1 * grads
        two = 0.95 * v_ref[:, at].astype(F32) + 0.05 * grads * grads
        direction = one / fix_one / (jnp.sqrt(two / fix_two) + 1e-08)
        master_out[:, at] = master - 0.001 * (direction + 0.1 * master)
        m_out[:, at] = one.astype(BF16)
        v_out[:, at] = two.astype(BF16)


def adam(opt, mine, recv, master, first_moment, second_moment):
    half = pl.BlockSpec((32, 896), lambda i, opt: (i, 0))
    whole = pl.BlockSpec((32, 1792), lambda i, opt: (i, 0))
    return pl.pallas_call(
        adam_kernel,
        out_shape=(
            jax.ShapeDtypeStruct((256, 1792), F32),
            jax.ShapeDtypeStruct((256, 1792), BF16),
            jax.ShapeDtypeStruct((256, 1792), BF16),
        ),
        grid_spec=pltpu.PrefetchScalarGridSpec(
            num_scalar_prefetch=1,
            grid=(8,),
            in_specs=[half, half, whole, whole, whole],
            out_specs=(whole, whole, whole),
        ),
        compiler_params=params(),
        cost_estimate=pl.CostEstimate(flops=256 * 1792 * 16, bytes_accessed=9 << 20, transcendentals=256 * 1792),
    )(opt, mine, recv, master, first_moment, second_moment)


def ring_gather(block):
    before, after = along_x(block, 1), along_x(block, -1)
    far0, far1 = along_x(before[:128], 1), along_x(after[128:], -1)
    return [block, before, after, far0, far1]


def body(tokens, grad_hidden, weight_codes, scales, master, first_moment, second_moment):
    o = lax.axis_index("opt")
    dp = lax.axis_index("dp")
    t = lax.axis_index("tensor")
    x, c = dp // 2, dp % 2
    zl, y = t // 4, t % 4
    z = o * 4 + zl
    opt = o.astype(jnp.int32).reshape(1)
    core = c.astype(jnp.int32).reshape(1)

    w_own, w_send = prepare(opt, scales, weight_codes)
    w_recv = other_opt(w_send)
    near = ring_gather(w_own)
    far = ring_gather(w_recv)

    keep, send = split_tokens(core, tokens)
    t_own = jnp.concatenate([keep, other_core(send)], axis=0)
    eighth = lax.dynamic_slice_in_dim(t_own, (t % 8) * 64, 64, axis=0)
    t_far = lax.all_gather(other_opt(eighth), "tensor", axis_index_groups=EIGHTHS, axis=0, tiled=True)

    lower = grad_hidden[:, :512]
    upper = jnp.concatenate([grad_hidden[:, 512:], grad_hidden[:, 448:512], grad_hidden[:, 384:448]], axis=1)
    up_own = jnp.where(o == 0, lower, upper)
    up_far = other_opt(jnp.where(o == 0, upper, lower))

    xs = [x, (x + 3) % 4, (x + 1) % 4, (x + 2) % 4]
    rows = [2 * v for v in xs] + [2 * xs[3] + 1]
    at = jnp.stack([o * 8 + v for v in rows] + [(1 - o) * 8 + v for v in rows]).astype(jnp.int32)

    own0, send0 = project(at, t_own, near + far)
    recv0 = other_core(send0)
    own1, send1 = project(at, t_far, near + far)
    recv1 = other_core(send1)
    hidden0, g0 = swiglu(own0, recv0, up_own)
    hidden1, g2 = swiglu(own1, recv1, up_far)
    hidden_recv = other_opt(hidden1)
    half0 = jnp.where(o == 0, hidden0, hidden_recv)
    half1 = jnp.where(o == 0, hidden_recv, hidden0)
    hidden = jnp.concatenate([half0[:, :448], half1[:, 384:448], half1[:, :384]], axis=1)
    g1, g3 = other_core(g0), other_core(g2)

    w_near, w_far = jnp.concatenate(near, axis=0), jnp.concatenate(far, axis=0)
    weights = [w_near, w_far, other_core(w_near), other_core(w_far)]

    def table(k):
        target = (y + k) % 4
        core_is = (target % 2 != c).astype(jnp.int32) * 2
        which, block = [], []
        for zt in range(4):
            xt = (zt % 2) * 2 + target // 2
            which.append(core_is + (zt // 2 != o).astype(jnp.int32))
            d = (xt - x) % 4
            block.append(jnp.where(d == 0, 0, jnp.where(d == 3, 1, jnp.where(d == 1, 2, 3))))
        return jnp.stack(which).astype(jnp.int32), jnp.stack(block).astype(jnp.int32)

    w2, b2 = table(2)
    w1, b1 = table(1)
    w3, b3 = table(3)
    w0, b0 = table(0)
    forth = along_y(token_grad(w2[:2], b2[:2], g0, g2, weights), 1)
    back = along_y(token_grad(w2[2:], b2[2:], g0, g2, weights), -1)
    swap = jnp.array([2, 3, 0, 1])
    right = along_y(token_grad(w1, b1, g0, g2, weights, forth), 1)
    left = along_y(token_grad(w3[swap], b3[swap], g0, g2, weights, back), -1)
    mine = token_grad(w0, b0, g0, g2, weights)

    def piece(k):
        zt = (z + k) % 8
        zlt, hi = zt % 4, (zt // 4 != o).astype(jnp.int32)

        def of(a, first):
            return lax.dynamic_slice(a, (first, hi * 256, 0), (1, 256, 256))[0].astype(F32)

        return of(mine, zlt) + of(right, zlt) + of(left, (zlt + 2) % 4)

    up = along_z(piece(4).astype(BF16), 1)
    down = along_z(piece(5).astype(BF16), -1)
    up = along_z((up.astype(F32) + piece(3)).astype(BF16), 1)
    down = along_z((down.astype(F32) + piece(6)).astype(BF16), -1)
    up = along_z((up.astype(F32) + piece(2)).astype(BF16), 1)
    down = along_z((down.astype(F32) + piece(7)).astype(BF16), -1)
    up = along_z((up.astype(F32) + piece(1)).astype(BF16), 1)
    grad_tokens = (piece(0) + up.astype(F32) + down.astype(F32)).astype(BF16)

    all_g = (g0, g1, g2, g3)
    dw_far = lax.psum_scatter(
        weight_grad(1 - opt, t_own, t_far, all_g), "dp", scatter_dimension=0, axis_index_groups=X_GROUPS, tiled=True
    )
    dw_own = lax.psum_scatter(
        weight_grad(opt, t_own, t_far, all_g), "dp", scatter_dimension=0, axis_index_groups=X_GROUPS, tiled=True
    )
    new_master, new_first, new_second = adam(opt, dw_own, other_opt(dw_far), master, first_moment, second_moment)
    return hidden, grad_tokens, new_master, new_first, new_second


def solution(mesh):
    rows = ("opt", "dp")
    in_specs = (
        P(rows, None),
        P(rows, "tensor"),
        P(rows, None, "tensor"),
        P(rows, "tensor"),
        P(rows, "tensor"),
        P(rows, "tensor"),
        P(rows, "tensor"),
    )
    out_specs = (P(rows, "tensor"),) * 5
    return jax.shard_map(body, mesh=mesh, in_specs=in_specs, out_specs=out_specs, check_vma=False)
```

```python
import functools

import jax
import jax.numpy as jnp
from jax import lax
from jax.experimental import pallas as pl
from jax.experimental.pallas import tpu as pltpu
from jax.sharding import PartitionSpec as P

F32 = jnp.float32
BF16 = jnp.bfloat16
OT = ("opt", "tensor")
VMEM = pl.BlockSpec(memory_space=pltpu.VMEM)
SMEM = pl.BlockSpec(memory_space=pltpu.SMEM)
LIMIT = 28 * 1024 * 1024
COST = pl.CostEstimate(flops=1, bytes_accessed=1 << 20, transcendentals=0)


X_GROUPS = [[0, 2, 4, 6], [1, 3, 5, 7]]
EIGHTHS = [list(range(8)), list(range(8, 16))]


def along_x(a, step):
    return lax.ppermute(a, "dp", [(x * 2 + c, (x + step) % 4 * 2 + c) for x in range(4) for c in range(2)])


def other_core(a):
    return lax.ppermute(a, "dp", [(i, i ^ 1) for i in range(8)])


def other_opt(a):
    return lax.ppermute(a, "opt", [(0, 1), (1, 0)])


def along_y(a, step):
    return lax.ppermute(a, "tensor", [(z * 4 + y, z * 4 + (y + step) % 4) for z in range(4) for y in range(4)])


def along_z(a, step):
    return lax.ppermute(a, OT, [(z * 4 + y, (z + step) % 8 * 4 + y) for z in range(8) for y in range(4)])


def params(limit=LIMIT):
    return pltpu.CompilerParams(vmem_limit_bytes=limit)


def low_lanes(shape):
    return lax.broadcasted_iota(jnp.int32, shape, 1) < 64


def prepare_kernel(opt_ref, scale_ref, code_ref, own_ref, send_ref):
    first = opt_ref[0] == 0
    low = low_lanes((128, 128))

    def put(rows, at, half0, half1):
        own_ref[rows, at : at + 128] = jnp.where(first, half0, half1).astype(BF16)
        send_ref[rows, at : at + 128] = jnp.where(first, half1, half0).astype(BF16)

    for b in range(2):
        rows = slice(b * 128, b * 128 + 128)

        def tile(j):
            return code_ref[b, :, j * 128 : j * 128 + 128].astype(F32) * scale_ref[b, j]

        for part in range(2):
            for j in range(3):
                put(rows, part * 384 + j * 128, tile(part * 7 + j), tile(part * 7 + 4 + j))
        gate, up = tile(3), tile(10)
        put(
            rows,
            768,
            jnp.where(low, gate, pltpu.roll(up, 64, 1)),
            jnp.where(low, pltpu.roll(gate, 64, 1), up),
        )


def prepare(opt, scales, codes):
    out = jax.ShapeDtypeStruct((256, 896), BF16)
    return pl.pallas_call(
        prepare_kernel,
        out_shape=(out, out),
        in_specs=[SMEM, SMEM, VMEM],
        out_specs=(VMEM, VMEM),
        compiler_params=params(),
        cost_estimate=COST,
    )(opt, scales, codes)


def split_kernel(core_ref, keep_in, send_in, keep_ref, send_ref):
    keep_ref[...] = keep_in[...]
    send_ref[...] = send_in[...]


def split_tokens(core, tokens):
    rows = tokens.shape[0]
    out = jax.ShapeDtypeStruct((rows, 2048), BF16)

    def block(column):
        return pl.BlockSpec((rows, 256), lambda i, core: (0, column(i, core[0])))

    return pl.pallas_call(
        split_kernel,
        out_shape=(out, out),
        grid_spec=pltpu.PrefetchScalarGridSpec(
            num_scalar_prefetch=1,
            grid=(8,),
            in_specs=[block(lambda i, c: 2 * i + c), block(lambda i, c: 2 * i + 1 - c)],
            out_specs=(block(lambda i, c: i), block(lambda i, c: i)),
        ),
        compiler_params=params(),
        cost_estimate=COST,
    )(core, tokens, tokens)


def joined_kernel(out_ref, pieces):
    for i, piece in enumerate(pieces):
        out_ref[i] = piece[...]


def near_kernel(at_ref, r0_ref, r1_ref, *refs):
    pieces, (total_ref, joined_ref) = refs[:-2], refs[-2:]
    joined_kernel(joined_ref, pieces)
    for half, tok in enumerate((r0_ref, r1_ref)):
        total = None
        for i in range(4):
            columns = pl.ds(pl.multiple_of(at_ref[i] * 256, 256), 256)
            term = jnp.dot(tok[:, columns], joined_ref[i], preferred_element_type=F32)
            total = term if total is None else total + term
        total_ref[half * 256 : half * 256 + 256] = total


def project_near(at, r0, r1, pieces):
    return pl.pallas_call(
        near_kernel,
        out_shape=(jax.ShapeDtypeStruct((512, 896), F32), jax.ShapeDtypeStruct((4, 256, 896), BF16)),
        in_specs=[SMEM] + [VMEM] * 6,
        out_specs=(VMEM, VMEM),
        compiler_params=params(),
        cost_estimate=COST,
    )(at, r0, r1, *pieces)


def far_kernel(at_ref, r0_ref, r1_ref, theirs_ref, total_ref, near_ref, *refs):
    pieces, (own_ref, send_ref, joined_ref) = refs[:-3], refs[-3:]
    joined_kernel(joined_ref, pieces)
    for k in range(4):
        total = total_ref[k * 256 : k * 256 + 256] if k < 2 else None
        for i in range(4 if k < 2 else 0, 8):
            columns = pl.ds(pl.multiple_of(at_ref[i] * 256, 256), 256)
            weights = near_ref if i < 4 else joined_ref
            if k < 2:
                tok = (r0_ref, r1_ref)[k][:, columns]
            else:
                tok = theirs_ref[:, k - 2, :, columns].reshape(256, 256)
            term = jnp.dot(tok, weights[i % 4], preferred_element_type=F32)
            total = term if total is None else total + term
        if k % 2 == 0:
            own_ref[k // 2] = total
        else:
            send_ref[k // 2] = total.astype(BF16)


def project_far(at, *args):
    return pl.pallas_call(
        far_kernel,
        out_shape=(
            jax.ShapeDtypeStruct((2, 256, 896), F32),
            jax.ShapeDtypeStruct((2, 256, 896), BF16),
            jax.ShapeDtypeStruct((4, 256, 896), BF16),
        ),
        in_specs=[SMEM] + [VMEM] * 9,
        out_specs=(VMEM, VMEM, VMEM),
        compiler_params=params(),
        cost_estimate=COST,
    )(at, *args)


def swiglu_kernel(*refs):
    own_ref, recv_ref, *up_grads, hidden0_ref, hidden1_ref, grad_ref = refs

    def parts(gate, up, upstream):
        s = 1.0 / (1.0 + jnp.exp(-gate))
        act = gate * s
        return act * up, upstream * up * s * (1.0 + gate * (1.0 - s)), upstream * act

    for half, (up_grad_ref, hidden_ref) in enumerate(zip(up_grads, (hidden0_ref, hidden1_ref))):

        def projected(at):
            return own_ref[half, :, at : at + 128] + recv_ref[half, :, at : at + 128].astype(F32)

        for j in range(3):
            at = j * 128
            hidden, grad_gate, grad_up = parts(
                projected(at), projected(384 + at), up_grad_ref[:, at : at + 128].astype(F32)
            )
            hidden_ref[:, at : at + 128] = hidden.astype(BF16)
            grad_ref[half, :, at : at + 128] = grad_gate.astype(BF16)
            grad_ref[half, :, 384 + at : 384 + at + 128] = grad_up.astype(BF16)
        mixed = projected(768)
        hidden, grad_gate, grad_up = parts(mixed, pltpu.roll(mixed, 64, 1), up_grad_ref[:, 384:512].astype(F32))
        hidden_ref[:, 384:512] = hidden.astype(BF16)
        grad_ref[half, :, 768:896] = jnp.where(
            low_lanes(mixed.shape), grad_gate, pltpu.roll(grad_up, 64, 1)
        ).astype(BF16)


def swiglu(*args):
    hidden = jax.ShapeDtypeStruct((256, 512), BF16)
    return pl.pallas_call(
        swiglu_kernel,
        out_shape=(hidden, hidden, jax.ShapeDtypeStruct((2, 256, 896), BF16)),
        in_specs=[VMEM] * 4,
        out_specs=(VMEM, VMEM, VMEM),
        compiler_params=params(),
        cost_estimate=COST,
    )(*args)


def token_grad_kernel(which_ref, block_ref, half_ref, g_ref, *refs):
    weights, out_refs = refs[:4], refs[4:]
    for k, out_ref in enumerate(out_refs):
        size = out_ref.shape[0]

        def step(j, _):
            i = k * size + j
            for a in range(4):

                @pl.when(which_ref[i] == a)
                def _():
                    out_ref[j] = lax.dot_general(
                        g_ref[half_ref[i]],
                        weights[a][block_ref[i]],
                        (((1,), (1,)), ((), ())),
                        preferred_element_type=F32,
                    ).astype(BF16)

            return 0

        lax.fori_loop(0, size, step, 0)


def token_grad(table, g, weights, outs):
    size = table[0].shape[0] // outs
    return pl.pallas_call(
        token_grad_kernel,
        out_shape=[jax.ShapeDtypeStruct((size, 256, 256), BF16)] * outs,
        in_specs=[SMEM] * 3 + [VMEM] * 5,
        out_specs=[VMEM] * outs,
        compiler_params=params(),
        cost_estimate=COST,
    )(*table, g, *weights)


def add_kernel(a_ref, b_ref, c_ref, d_ref, ab_ref, cd_ref):
    ab_ref[...] = (a_ref[...].astype(F32) + b_ref[...].astype(F32)).astype(BF16)
    cd_ref[...] = (c_ref[...].astype(F32) + d_ref[...].astype(F32)).astype(BF16)


def add_parts(right, forth, left, back):
    first = pl.BlockSpec((1, 256, 256), lambda i: (i, 0, 0))
    second = pl.BlockSpec((1, 256, 256), lambda i: (i + 4, 0, 0))
    out = jax.ShapeDtypeStruct((8, 256, 256), BF16)
    return pl.pallas_call(
        add_kernel,
        out_shape=(out, out),
        grid=(4,),
        in_specs=[first, first, second, first],
        out_specs=(first, second),
        input_output_aliases={0: 0, 2: 1},
        compiler_params=params(),
        cost_estimate=COST,
    )(right, forth, left, back)


def weight_grad_kernel(half_ref, r0, r1, theirs, g_ref, h_ref, out_ref):
    for k in range(4):
        columns = pl.ds(pl.multiple_of((half_ref[0] * 4 + k) * 256, 256), 256)
        total = None
        for t, g in (
            (r0[:, columns], g_ref[0]),
            (r1[:, columns], h_ref[0]),
            (theirs[:, 0, :, columns].reshape(256, 256), g_ref[1]),
            (theirs[:, 1, :, columns].reshape(256, 256), h_ref[1]),
        ):
            term = lax.dot_general(t, g, (((0,), (0,)), ((), ())), preferred_element_type=F32)
            total = term if total is None else total + term
        out_ref[k * 256 : k * 256 + 256] = (total * (1.0 / 64.0)).astype(BF16)


def weight_grad(half, *args):
    return pl.pallas_call(
        weight_grad_kernel,
        out_shape=jax.ShapeDtypeStruct((1024, 896), BF16),
        in_specs=[SMEM] + [VMEM] * 5,
        out_specs=VMEM,
        compiler_params=params(),
        cost_estimate=COST,
    )(half, *args)


def sum_over_x(d):
    return lax.psum_scatter(d, "dp", scatter_dimension=0, axis_index_groups=X_GROUPS, tiled=True)


def adam_kernel(opt_ref, *refs):
    mine_ref, recv_ref, hidden_ref, theirs_ref, master_ref, m_ref, v_ref = refs[:7]
    master_out, m_out, v_out, hidden_out = refs[7:]
    first = opt_ref[0] == 0
    low = low_lanes((recv_ref.shape[0], 128))
    fix_one = 1.0 - 0.9**20.0
    fix_two = 1.0 - 0.95**20.0

    def pick(half, mine, recv):
        return jnp.where(first, mine, recv) if half == 0 else jnp.where(first, recv, mine)

    def tile(half, at):
        return pick(half, mine_ref[:, at : at + 128].astype(F32), recv_ref[:, at : at + 128].astype(F32))

    def hidden_tile(half, at):
        recv = theirs_ref[:, at : at + 128].astype(F32)
        return pick(half, hidden_ref[:, at : at + 128].astype(F32), recv)

    mixed0, mixed1 = tile(0, 768), tile(1, 768)
    for j in range(14):
        part, k = divmod(j, 7)
        if k < 3:
            grads = tile(0, part * 384 + k * 128)
        elif k > 3:
            grads = tile(1, part * 384 + (k - 4) * 128)
        elif part == 0:
            grads = jnp.where(low, mixed0, pltpu.roll(mixed1, 64, 1))
        else:
            grads = jnp.where(low, pltpu.roll(mixed0, 64, 1), mixed1)
        at = slice(j * 128, j * 128 + 128)
        master = master_ref[:, at]
        one = 0.9 * m_ref[:, at].astype(F32) + 0.1 * grads
        two = 0.95 * v_ref[:, at].astype(F32) + 0.05 * grads * grads
        direction = one / fix_one / (jnp.sqrt(two / fix_two) + 1e-08)
        master_out[:, at] = master - 0.001 * (direction + 0.1 * master)
        m_out[:, at] = one.astype(BF16)
        v_out[:, at] = two.astype(BF16)
    for k in range(7):
        if k < 3:
            hidden = hidden_tile(0, k * 128)
        elif k > 3:
            hidden = hidden_tile(1, (k - 4) * 128)
        else:
            hidden = jnp.where(low, hidden_tile(0, 384), pltpu.roll(hidden_tile(1, 384), 64, 1))
        hidden_out[:, k * 128 : k * 128 + 128] = hidden.astype(BF16)


def adam(opt, *args):
    def rows(width):
        return pl.BlockSpec((32, width), lambda i, opt: (i, 0))

    return pl.pallas_call(
        adam_kernel,
        out_shape=(
            jax.ShapeDtypeStruct((256, 1792), F32),
            jax.ShapeDtypeStruct((256, 1792), BF16),
            jax.ShapeDtypeStruct((256, 1792), BF16),
            jax.ShapeDtypeStruct((256, 896), BF16),
        ),
        grid_spec=pltpu.PrefetchScalarGridSpec(
            num_scalar_prefetch=1,
            grid=(8,),
            in_specs=[rows(896)] * 2 + [rows(512)] * 2 + [rows(1792)] * 3,
            out_specs=(rows(1792), rows(1792), rows(1792), rows(896)),
        ),
        compiler_params=params(60 * 1024 * 1024),
        cost_estimate=COST,
    )(opt, *args)


def gather_x(block):
    return [block, along_x(block, 1), along_x(block, -1), along_x(block, 2)]


def body(tokens, grad_hidden, weight_codes, scales, master, first_moment, second_moment):
    o = lax.axis_index("opt")
    dp = lax.axis_index("dp")
    t = lax.axis_index("tensor")
    x, c = dp // 2, dp % 2
    zl, y = t // 4, t % 4
    z = o * 4 + zl
    opt = o.astype(jnp.int32).reshape(1)
    core = c.astype(jnp.int32).reshape(1)
    barrier = lax.optimization_barrier

    eighth = other_opt(lax.dynamic_slice_in_dim(tokens, (t % 8) * 32, 32, axis=0))
    r0, send = split_tokens(core, tokens)
    w_own, w_send = prepare(opt, scales, weight_codes)
    eighth, r0, send, w_own, w_send = barrier((eighth, r0, send, w_own, w_send))
    r1 = other_core(send)
    keep, part = split_tokens(core, eighth)
    theirs = lax.all_gather(jnp.stack([keep, other_core(part)]), "tensor", axis_index_groups=EIGHTHS)

    *near, w_recv = barrier((*gather_x(w_own), other_opt(w_send)))
    far = gather_x(w_recv)

    lower = grad_hidden[:, :512]
    upper = jnp.concatenate([grad_hidden[:, 512:], grad_hidden[:, 448:512], grad_hidden[:, 384:448]], axis=1)
    up_own = jnp.where(o == 0, lower, upper)
    up_send, _ = barrier((jnp.where(o == 0, upper, lower), w_recv))
    up_far = other_opt(up_send)

    xs = jnp.stack([x, (x + 3) % 4, (x + 1) % 4, (x + 2) % 4])
    at_near = (o * 4 + xs).astype(jnp.int32)
    at_far = ((1 - o) * 4 + xs).astype(jnp.int32)
    total, w_near = project_near(at_near, r0, r1, near)
    total, up_far, *far = barrier((total, up_far, *far))
    own, send, w_far = project_far(jnp.concatenate([at_near, at_far]), r0, r1, theirs, total, w_near, *far)
    recv, w_near_other = barrier((other_core(send), other_core(w_near)))
    hidden0, hidden1, g = swiglu(own, recv, up_own, up_far)
    g, w_far_other = barrier((g, other_core(w_far)))
    g_other = other_core(g)
    weights = [w_near, w_far, w_near_other, w_far_other]

    def table(*targets):
        which, block, half = [], [], []
        for ky, kz in targets:
            yt, zt = (y + ky) % 4, (z + kz) % 8
            zlt = zt % 4
            d = ((zlt % 2) * 2 + yt // 2 - x) % 4
            which.append(jnp.where(yt % 2 == c, 0, 2) + jnp.where(zlt // 2 == o, 0, 1))
            block.append(jnp.where(d == 0, 0, jnp.where(d == 3, 1, jnp.where(d == 1, 2, 3))))
            half.append(jnp.where(zt // 4 == o, 0, 1))
        return [jnp.stack(v).astype(jnp.int32) for v in (which, block, half)]

    def targets(*kys):
        return [(ky, kz) for ky in kys for kz in range(8)]

    forth, back = token_grad(table(*targets(2)), g, weights, 2)
    g, g_other, _ = barrier((g, g_other, forth))
    forth, back = along_y(forth, 1), along_y(back, -1)
    dw_far = weight_grad(1 - opt, r0, r1, theirs, g, g_other)
    g, g_other, _ = barrier((g, g_other, dw_far))
    right, left, mine = token_grad(table(*targets(1, 3, 0)), g, weights, 3)
    hidden_recv = other_opt(hidden1)
    forth, back, right, left, g, hidden_recv = barrier((forth, back, right, left, g, hidden_recv))
    right, left = add_parts(right, forth, left, back)
    right, left = along_y(right, 1), along_y(left, -1)
    dw_own = weight_grad(opt, r0, r1, theirs, g, g_other)
    dw_far, dw_own = sum_over_x(dw_far), sum_over_x(dw_own)
    right, left, mine, dw_recv = barrier((right, left, mine, other_opt(dw_far)))

    def piece(kz):
        return sum(a[kz].astype(F32) for a in (mine, right, left))

    up = along_z(piece(4).astype(BF16), 1)
    down = along_z(piece(5).astype(BF16), -1)
    updated = adam(opt, dw_own, dw_recv, hidden0, hidden_recv, master, first_moment, second_moment)
    up, down, *updated = barrier((up, down, *updated))
    up = along_z((up.astype(F32) + piece(3)).astype(BF16), 1)
    down = along_z((down.astype(F32) + piece(6)).astype(BF16), -1)
    up = along_z((up.astype(F32) + piece(2)).astype(BF16), 1)
    down = along_z((down.astype(F32) + piece(7)).astype(BF16), -1)
    up = along_z((up.astype(F32) + piece(1)).astype(BF16), 1)
    grad_tokens = (piece(0) + up.astype(F32) + down.astype(F32)).astype(BF16)
    new_master, new_first, new_second, hidden = updated
    return hidden, grad_tokens, new_master, new_first, new_second


def solution(mesh):
    rows = ("opt", "dp")
    in_specs = (
        P(rows, None),
        P(rows, "tensor"),
        P(rows, None, "tensor"),
        P(rows, "tensor"),
        P(rows, "tensor"),
        P(rows, "tensor"),
        P(rows, "tensor"),
    )
    out_specs = (P(rows, "tensor"),) * 5
    return jax.shard_map(body, mesh=mesh, in_specs=in_specs, out_specs=out_specs, check_vma=False)
```

```python
import functools

import jax
import jax.numpy as jnp
from jax import lax
from jax.experimental import pallas as pl
from jax.experimental.pallas import tpu as pltpu
from jax.sharding import PartitionSpec as P

F32 = jnp.float32
BF16 = jnp.bfloat16
OT = ("opt", "tensor")
VMEM = pl.BlockSpec(memory_space=pltpu.VMEM)
SMEM = pl.BlockSpec(memory_space=pltpu.SMEM)
LIMIT = 28 * 1024 * 1024
COST = pl.CostEstimate(flops=1, bytes_accessed=1 << 20, transcendentals=0)


X_GROUPS = [[0, 2, 4, 6], [1, 3, 5, 7]]
EIGHTHS = [list(range(8)), list(range(8, 16))]


def along_x(a, step):
    return lax.ppermute(a, "dp", [(x * 2 + c, (x + step) % 4 * 2 + c) for x in range(4) for c in range(2)])


def other_core(a):
    return lax.ppermute(a, "dp", [(i, i ^ 1) for i in range(8)])


def other_opt(a):
    return lax.ppermute(a, "opt", [(0, 1), (1, 0)])


def along_y(a, step):
    return lax.ppermute(a, "tensor", [(z * 4 + y, z * 4 + (y + step) % 4) for z in range(4) for y in range(4)])


def along_z(a, step):
    return lax.ppermute(a, OT, [(z * 4 + y, (z + step) % 8 * 4 + y) for z in range(8) for y in range(4)])


def params(limit=LIMIT):
    return pltpu.CompilerParams(vmem_limit_bytes=limit)


def low_lanes(shape):
    return lax.broadcasted_iota(jnp.int32, shape, 1) < 64


def prepare_kernel(opt_ref, scale_ref, code_ref, own_ref, send_ref):
    first = opt_ref[0] == 0
    low = low_lanes((128, 128))

    def put(rows, at, half0, half1):
        own_ref[rows, at : at + 128] = jnp.where(first, half0, half1).astype(BF16)
        send_ref[rows, at : at + 128] = jnp.where(first, half1, half0).astype(BF16)

    for b in range(2):
        rows = slice(b * 128, b * 128 + 128)

        def tile(j):
            return code_ref[b, :, j * 128 : j * 128 + 128].astype(F32) * scale_ref[b, j]

        for part in range(2):
            for j in range(3):
                put(rows, part * 384 + j * 128, tile(part * 7 + j), tile(part * 7 + 4 + j))
        gate, up = tile(3), tile(10)
        put(
            rows,
            768,
            jnp.where(low, gate, pltpu.roll(up, 64, 1)),
            jnp.where(low, pltpu.roll(gate, 64, 1), up),
        )


def prepare(opt, scales, codes):
    out = jax.ShapeDtypeStruct((256, 896), BF16)
    return pl.pallas_call(
        prepare_kernel,
        out_shape=(out, out),
        in_specs=[SMEM, SMEM, VMEM],
        out_specs=(VMEM, VMEM),
        compiler_params=params(),
        cost_estimate=COST,
    )(opt, scales, codes)


def split_kernel(core_ref, keep_in, send_in, keep_ref, send_ref):
    keep_ref[...] = keep_in[...]
    send_ref[...] = send_in[...]


def split_tokens(core, tokens):
    rows = tokens.shape[0]
    out = jax.ShapeDtypeStruct((rows, 2048), BF16)

    def block(column):
        return pl.BlockSpec((rows, 256), lambda i, core: (0, column(i, core[0])))

    return pl.pallas_call(
        split_kernel,
        out_shape=(out, out),
        grid_spec=pltpu.PrefetchScalarGridSpec(
            num_scalar_prefetch=1,
            grid=(8,),
            in_specs=[block(lambda i, c: 2 * i + c), block(lambda i, c: 2 * i + 1 - c)],
            out_specs=(block(lambda i, c: i), block(lambda i, c: i)),
        ),
        compiler_params=params(),
        cost_estimate=COST,
    )(core, tokens, tokens)


def joined_kernel(out_ref, pieces):
    for i, piece in enumerate(pieces):
        out_ref[i] = piece[...]


def near_kernel(at_ref, r0_ref, r1_ref, *refs):
    pieces, (total_ref, joined_ref) = refs[:-2], refs[-2:]
    joined_kernel(joined_ref, pieces)
    for half, tok in enumerate((r0_ref, r1_ref)):
        total = None
        for i in range(4):
            columns = pl.ds(pl.multiple_of(at_ref[i] * 256, 256), 256)
            term = jnp.dot(tok[:, columns], joined_ref[i], preferred_element_type=F32)
            total = term if total is None else total + term
        total_ref[half * 256 : half * 256 + 256] = total


def project_near(at, r0, r1, pieces):
    return pl.pallas_call(
        near_kernel,
        out_shape=(jax.ShapeDtypeStruct((512, 896), F32), jax.ShapeDtypeStruct((4, 256, 896), BF16)),
        in_specs=[SMEM] + [VMEM] * 6,
        out_specs=(VMEM, VMEM),
        compiler_params=params(),
        cost_estimate=COST,
    )(at, r0, r1, *pieces)


def far_kernel(at_ref, r0_ref, r1_ref, theirs_ref, total_ref, near_ref, *refs):
    pieces, (own_ref, send_ref, joined_ref) = refs[:-3], refs[-3:]
    joined_kernel(joined_ref, pieces)
    for k in range(4):
        total = total_ref[k * 256 : k * 256 + 256] if k < 2 else None
        for i in range(4 if k < 2 else 0, 8):
            columns = pl.ds(pl.multiple_of(at_ref[i] * 256, 256), 256)
            weights = near_ref if i < 4 else joined_ref
            if k < 2:
                tok = (r0_ref, r1_ref)[k][:, columns]
            else:
                tok = theirs_ref[:, k - 2, :, columns].reshape(256, 256)
            term = jnp.dot(tok, weights[i % 4], preferred_element_type=F32)
            total = term if total is None else total + term
        if k % 2 == 0:
            own_ref[k // 2] = total
        else:
            send_ref[k // 2] = total.astype(BF16)


def project_far(at, *args):
    return pl.pallas_call(
        far_kernel,
        out_shape=(
            jax.ShapeDtypeStruct((2, 256, 896), F32),
            jax.ShapeDtypeStruct((2, 256, 896), BF16),
            jax.ShapeDtypeStruct((4, 256, 896), BF16),
        ),
        in_specs=[SMEM] + [VMEM] * 9,
        out_specs=(VMEM, VMEM, VMEM),
        compiler_params=params(),
        cost_estimate=COST,
    )(at, *args)


def swiglu_kernel(*refs):
    own_ref, recv_ref, *up_grads, hidden0_ref, hidden1_ref, grad_ref = refs

    def parts(gate, up, upstream):
        s = 1.0 / (1.0 + jnp.exp(-gate))
        act = gate * s
        return act * up, upstream * up * s * (1.0 + gate * (1.0 - s)), upstream * act

    for half, (up_grad_ref, hidden_ref) in enumerate(zip(up_grads, (hidden0_ref, hidden1_ref))):

        def projected(at):
            return own_ref[half, :, at : at + 128] + recv_ref[half, :, at : at + 128].astype(F32)

        for j in range(3):
            at = j * 128
            hidden, grad_gate, grad_up = parts(
                projected(at), projected(384 + at), up_grad_ref[:, at : at + 128].astype(F32)
            )
            hidden_ref[:, at : at + 128] = hidden.astype(BF16)
            grad_ref[half, :, at : at + 128] = grad_gate.astype(BF16)
            grad_ref[half, :, 384 + at : 384 + at + 128] = grad_up.astype(BF16)
        mixed = projected(768)
        hidden, grad_gate, grad_up = parts(mixed, pltpu.roll(mixed, 64, 1), up_grad_ref[:, 384:512].astype(F32))
        hidden_ref[:, 384:512] = hidden.astype(BF16)
        grad_ref[half, :, 768:896] = jnp.where(
            low_lanes(mixed.shape), grad_gate, pltpu.roll(grad_up, 64, 1)
        ).astype(BF16)


def swiglu(*args):
    hidden = jax.ShapeDtypeStruct((256, 512), BF16)
    return pl.pallas_call(
        swiglu_kernel,
        out_shape=(hidden, hidden, jax.ShapeDtypeStruct((2, 256, 896), BF16)),
        in_specs=[VMEM] * 4,
        out_specs=(VMEM, VMEM, VMEM),
        compiler_params=params(),
        cost_estimate=COST,
    )(*args)


def token_grad_kernel(which_ref, block_ref, half_ref, g_ref, *refs):
    weights, out_refs = refs[:4], refs[4:]
    first = 0
    for out_ref in out_refs:

        def step(j, _, out_ref=out_ref, first=first):
            i = first + j
            for a in range(4):

                @pl.when(which_ref[i] == a)
                def _():
                    out_ref[j] = lax.dot_general(
                        g_ref[half_ref[i]],
                        weights[a][block_ref[i]],
                        (((1,), (1,)), ((), ())),
                        preferred_element_type=F32,
                    ).astype(BF16)

            return 0

        lax.fori_loop(0, out_ref.shape[0], step, 0)
        first += out_ref.shape[0]


def token_grad(table, g, weights, sizes):
    return pl.pallas_call(
        token_grad_kernel,
        out_shape=[jax.ShapeDtypeStruct((n, 256, 256), BF16) for n in sizes],
        in_specs=[SMEM] * 3 + [VMEM] * 5,
        out_specs=[VMEM] * len(sizes),
        compiler_params=params(),
        cost_estimate=COST,
    )(*table, g, *weights)


def add_kernel(a_ref, b_ref, c_ref, d_ref, ab_ref, cd_ref):
    ab_ref[...] = (a_ref[...].astype(F32) + b_ref[...].astype(F32)).astype(BF16)
    cd_ref[...] = (c_ref[...].astype(F32) + d_ref[...].astype(F32)).astype(BF16)


def add_parts(*args):
    out = jax.ShapeDtypeStruct((4, 256, 256), BF16)
    return pl.pallas_call(
        add_kernel,
        out_shape=(out, out),
        in_specs=[VMEM] * 4,
        out_specs=(VMEM, VMEM),
        compiler_params=params(),
        cost_estimate=COST,
    )(*args)


def weight_grad_kernel(opt_ref, r0, r1, theirs, g_ref, h_ref, *outs):
    for n, out_ref in enumerate(outs):
        group = 1 - opt_ref[0] if n == 0 else opt_ref[0]
        for k in range(4):
            columns = pl.ds(pl.multiple_of((group * 4 + k) * 256, 256), 256)
            total = None
            for t, g in (
                (r0[:, columns], g_ref[0]),
                (r1[:, columns], h_ref[0]),
                (theirs[:, 0, :, columns].reshape(256, 256), g_ref[1]),
                (theirs[:, 1, :, columns].reshape(256, 256), h_ref[1]),
            ):
                term = lax.dot_general(t, g, (((0,), (0,)), ((), ())), preferred_element_type=F32)
                total = term if total is None else total + term
            out_ref[k * 256 : k * 256 + 256] = (total * (1.0 / 64.0)).astype(BF16)


def weight_grad(opt, *args):
    return pl.pallas_call(
        weight_grad_kernel,
        out_shape=[jax.ShapeDtypeStruct((1024, 896), BF16)] * 2,
        in_specs=[SMEM] + [VMEM] * 5,
        out_specs=[VMEM] * 2,
        compiler_params=params(),
        cost_estimate=COST,
    )(opt, *args)


def sum_over_x(d):
    return lax.psum_scatter(d, "dp", scatter_dimension=0, axis_index_groups=X_GROUPS, tiled=True)


def adam_kernel(opt_ref, *refs):
    mine_ref, recv_ref, hidden_ref, theirs_ref, master_ref, m_ref, v_ref = refs[:7]
    master_out, m_out, v_out, hidden_out = refs[7:]
    first = opt_ref[0] == 0
    low = low_lanes((recv_ref.shape[0], 128))
    fix_one = 1.0 - 0.9**20.0
    fix_two = 1.0 - 0.95**20.0

    def pick(half, mine, recv):
        return jnp.where(first, mine, recv) if half == 0 else jnp.where(first, recv, mine)

    def tile(half, at):
        return pick(half, mine_ref[:, at : at + 128].astype(F32), recv_ref[:, at : at + 128].astype(F32))

    def hidden_tile(half, at):
        recv = theirs_ref[:, at : at + 128].astype(F32)
        return pick(half, hidden_ref[:, at : at + 128].astype(F32), recv)

    mixed0, mixed1 = tile(0, 768), tile(1, 768)
    for j in range(14):
        part, k = divmod(j, 7)
        if k < 3:
            grads = tile(0, part * 384 + k * 128)
        elif k > 3:
            grads = tile(1, part * 384 + (k - 4) * 128)
        elif part == 0:
            grads = jnp.where(low, mixed0, pltpu.roll(mixed1, 64, 1))
        else:
            grads = jnp.where(low, pltpu.roll(mixed0, 64, 1), mixed1)
        at = slice(j * 128, j * 128 + 128)
        master = master_ref[:, at]
        one = 0.9 * m_ref[:, at].astype(F32) + 0.1 * grads
        two = 0.95 * v_ref[:, at].astype(F32) + 0.05 * grads * grads
        direction = one * (1.0 / fix_one) / (jnp.sqrt(two * (1.0 / fix_two)) + 1e-08)
        master_out[:, at] = master - 0.001 * (direction + 0.1 * master)
        m_out[:, at] = one.astype(BF16)
        v_out[:, at] = two.astype(BF16)
    for k in range(7):
        if k < 3:
            hidden = hidden_tile(0, k * 128)
        elif k > 3:
            hidden = hidden_tile(1, (k - 4) * 128)
        else:
            hidden = jnp.where(low, hidden_tile(0, 384), pltpu.roll(hidden_tile(1, 384), 64, 1))
        hidden_out[:, k * 128 : k * 128 + 128] = hidden.astype(BF16)


def adam(opt, *args):
    def rows(width):
        return pl.BlockSpec((64, width), lambda i, opt: (i, 0))

    return pl.pallas_call(
        adam_kernel,
        out_shape=(
            jax.ShapeDtypeStruct((256, 1792), F32),
            jax.ShapeDtypeStruct((256, 1792), BF16),
            jax.ShapeDtypeStruct((256, 1792), BF16),
            jax.ShapeDtypeStruct((256, 896), BF16),
        ),
        grid_spec=pltpu.PrefetchScalarGridSpec(
            num_scalar_prefetch=1,
            grid=(4,),
            in_specs=[rows(896)] * 2 + [rows(512)] * 2 + [rows(1792)] * 3,
            out_specs=(rows(1792), rows(1792), rows(1792), rows(896)),
        ),
        compiler_params=params(60 * 1024 * 1024),
        cost_estimate=COST,
    )(opt, *args)


def gather_x(block):
    return [block, along_x(block, 1), along_x(block, -1), along_x(block, 2)]


def body(tokens, grad_hidden, weight_codes, scales, master, first_moment, second_moment):
    o = lax.axis_index("opt")
    dp = lax.axis_index("dp")
    t = lax.axis_index("tensor")
    x, c = dp // 2, dp % 2
    zl, y = t // 4, t % 4
    z = o * 4 + zl
    opt = o.astype(jnp.int32).reshape(1)
    core = c.astype(jnp.int32).reshape(1)
    barrier = lax.optimization_barrier

    eighth = other_opt(lax.dynamic_slice_in_dim(tokens, (t % 8) * 32, 32, axis=0))
    r0, send = split_tokens(core, tokens)
    w_own, w_send = prepare(opt, scales, weight_codes)
    eighth, r0, send, w_own, w_send = barrier((eighth, r0, send, w_own, w_send))
    r1 = other_core(send)
    keep, part = split_tokens(core, eighth)
    theirs = lax.all_gather(jnp.stack([keep, other_core(part)]), "tensor", axis_index_groups=EIGHTHS)

    *near, w_recv = barrier((*gather_x(w_own), other_opt(w_send)))
    far = gather_x(w_recv)

    lower = grad_hidden[:, :512]
    upper = jnp.concatenate([grad_hidden[:, 512:], grad_hidden[:, 448:512], grad_hidden[:, 384:448]], axis=1)
    up_own = jnp.where(o == 0, lower, upper)
    up_send, _ = barrier((jnp.where(o == 0, upper, lower), w_recv))
    up_far = other_opt(up_send)

    xs = jnp.stack([x, (x + 3) % 4, (x + 1) % 4, (x + 2) % 4])
    at_near = (o * 4 + xs).astype(jnp.int32)
    at_far = ((1 - o) * 4 + xs).astype(jnp.int32)
    total, w_near = project_near(at_near, r0, r1, near)
    total, up_far, *far = barrier((total, up_far, *far))
    own, send, w_far = project_far(jnp.concatenate([at_near, at_far]), r0, r1, theirs, total, w_near, *far)
    recv, w_near_other = barrier((other_core(send), other_core(w_near)))
    hidden0, hidden1, g = swiglu(own, recv, up_own, up_far)
    g, w_far_other = barrier((g, other_core(w_far)))
    g_other = other_core(g)
    weights = [w_near, w_far, w_near_other, w_far_other]

    def table(*targets):
        which, block, half = [], [], []
        for ky, kz in targets:
            yt, zt = (y + ky) % 4, (z + kz) % 8
            zlt = zt % 4
            d = ((zlt % 2) * 2 + yt // 2 - x) % 4
            which.append(jnp.where(yt % 2 == c, 0, 2) + jnp.where(zlt // 2 == o, 0, 1))
            block.append(jnp.where(d == 0, 0, jnp.where(d == 3, 1, jnp.where(d == 1, 2, 3))))
            half.append(jnp.where(zt // 4 == o, 0, 1))
        return [jnp.stack(v).astype(jnp.int32) for v in (which, block, half)]

    chunk1, chunk2 = (4, 5, 3, 6), (2, 7, 1, 0)

    def targets(*parts):
        return [(ky, kz) for ky, chunk in parts for kz in chunk]

    hidden_recv = other_opt(hidden1)
    dw_far, dw_own = weight_grad(opt, r0, r1, theirs, g, g_other)
    g, _ = barrier((g, dw_far))
    dw_far, dw_own = sum_over_x(dw_far), sum_over_x(dw_own)
    forth, back = token_grad(table(*targets((2, chunk1), (2, chunk2))), g, weights, (4, 4))
    g, forth, back, hidden_recv = barrier((g, forth, back, hidden_recv))
    forth, back = along_y(forth, 1), along_y(back, -1)
    every = targets((1, chunk1), (1, chunk2), (3, chunk1), (3, chunk2), (0, chunk1), (0, chunk2))
    right1, right2, left1, left2, mine = token_grad(table(*every), g, weights, (4, 4, 4, 4, 8))
    forth, back, right1, right2, left1, left2, mine = barrier((forth, back, right1, right2, left1, left2, mine))
    right1, left2 = add_parts(right1, forth, left2, back)
    right1, left1 = along_y(right1, 1), along_y(left1, -1)
    right2, left2 = along_y(right2, 1), along_y(left2, -1)
    dw_recv = other_opt(dw_far)

    def piece(i):
        right, left = (right1, left1) if i < 4 else (right2, left2)
        return mine[i].astype(F32) + right[i % 4].astype(F32) + left[i % 4].astype(F32)

    right1, left1, dw_recv = barrier((right1, left1, dw_recv))
    terms = [along_z(piece(i).astype(BF16), kz) for i, kz in enumerate((chunk1 + chunk2)[:7])]
    updated = adam(opt, dw_own, dw_recv, hidden0, hidden_recv, master, first_moment, second_moment)
    *terms, updated = barrier((*terms, updated))
    grad_tokens = (piece(7) + sum(a.astype(F32) for a in terms)).astype(BF16)
    new_master, new_first, new_second, hidden = updated
    return hidden, grad_tokens, new_master, new_first, new_second


def solution(mesh):
    rows = ("opt", "dp")
    in_specs = (
        P(rows, None),
        P(rows, "tensor"),
        P(rows, None, "tensor"),
        P(rows, "tensor"),
        P(rows, "tensor"),
        P(rows, "tensor"),
        P(rows, "tensor"),
    )
    out_specs = (P(rows, "tensor"),) * 5
    return jax.shard_map(body, mesh=mesh, in_specs=in_specs, out_specs=out_specs, check_vma=False)
```
